512 devices in a mesh: row: 16 (over x, y_lo, core), col: 32 (over y_hi, z).
Axes of the slice: x: 4, y: 8 (y_hi: 4, y_lo: 2; y = y_hi * 2 + y_lo), z: 8, core: 2. Of those that a mesh axis runs over, the one named last changes fastest.
Arguments:
- iterate: bfloat16 [4096, 18432], P('row', 'col'), may hold values from -0.03125 to 0.03125
Outputs:
- update: bfloat16 [4096, 18432], P('row', 'col')
The draws below stay inside these ranges and needn't reach their ends.
All inputs are finite; a program needn't handle non-finite values.
Results may differ from the reference program's by a relative error of at most 0.006.
Values may be sent and summed in bfloat16 or wider, within the bound.
No kernel may reach another device: no remote copies, remote signals or barrier semaphores. Data moves between devices by JAX's collectives and lax.ppermute only.
A program may use at most 64 MiB of HBM per device.

```python
import math
import jax
import jax.numpy as jnp

ROWS = 4096
COLS = 18432


def steps_of(rng, dims, split, low, high):
    def one(position, parts):
        heights = jax.random.uniform(jax.random.fold_in(jax.random.fold_in(rng, 6), position), (parts,), jnp.float32, low / len(split), high / len(split))
        return jnp.repeat(jnp.exp(heights), dims[position] // parts).reshape((-1,) + (1,) * (len(dims) - position - 1))

    gain = one(*split[0])
    for cut in split[1:]:
        gain = gain * one(*cut)
    return gain


def scatter_about(key, shape, scale, most, shards=(), kind=jnp.bfloat16):
    array = jax.random.normal(key, shape, jnp.float32) * scale
    if len(shards) > 0:
        array = steps_of(key, shape, shards, -0.22, 0.18) * array
    return jnp.clip(array, min=-most, max=most).astype(kind)


def setup_inputs(seed: int = 0) -> dict:
    arg_keys = jax.random.split(jax.random.key(seed), 2)
    return {
        "iterate": scatter_about(arg_keys[0], (ROWS, COLS), (COLS + ROWS * 4) ** -0.5, 0.03125, ((0, 16), (1, 32))),
    }


coef_linear = 3.4445
coef_cubic = -4.775
coef_quintic = 2.0315

def reference(iterate):
    gram = jnp.dot(iterate, iterate.T, preferred_element_type=jnp.float32).astype(jnp.bfloat16)
    squared = jnp.dot(gram, gram, preferred_element_type=jnp.float32)
    mixed = (coef_cubic * gram.astype(jnp.float32) + coef_quintic * squared).astype(jnp.bfloat16)
    product = jnp.dot(mixed, iterate, preferred_element_type=jnp.float32)
    update_scale = 0.2 * math.sqrt(max(ROWS, COLS))
    update = update_scale * (coef_linear * iterate.astype(jnp.float32) + product)
    return update.astype(jnp.bfloat16)
```

```python
import math

import jax
import jax.numpy as jnp
from jax import lax
from jax.experimental import pallas as pl
from jax.experimental.pallas import tpu as pltpu
from jax.sharding import Mesh, PartitionSpec as P

coef_linear = 3.4445
coef_cubic = -4.775
coef_quintic = 2.0315

X, YL, CORE, YH, Z = 4, 2, 2, 4, 8
COL = ("yh", "z")
f32 = jnp.float32
bf16 = jnp.bfloat16

BLOCKS = 9
PIECE = 16


def shift(value, axis, size, by):
    return lax.ppermute(value, axis, [(i, (i + by) % size) for i in range(size)])


def dot(a, b, ca, cb):
    return lax.dot_general(a, b, (((ca,), (cb,)), ((), ())), preferred_element_type=f32)


def gram_kernel(flag, a0m, a0o, a1m, a2m, a2o, a3m, a3o, out):
    f2, f3 = flag[0] == 1, flag[1] == 1
    n = a0m.shape[1]
    a2f = jnp.where(f2, a2o[...], a2m[...])
    a3f = jnp.where(f3, a3o[...], a3m[...])
    pairs = [
        (a1m, a0m), (a1m, a0o), (a1m, a3m), (a1m, a3o),
        (a0m, a2f), (a0m, a3f), (a2m, a3f), (a0m, a0m), (a0m, a0o),
    ]
    for i, (a, b) in enumerate(pairs):
        block = dot(a[...], b[...], 0, 0).astype(bf16)
        for h in range(2):
            half = block[:, h * 128:(h + 1) * 128]
            out[h * 16:(h + 1) * 16, i * PIECE:(i + 1) * PIECE, :] = half.reshape(n // PIECE, PIECE, 128)


def apply_kernel(flag, gm, go, a0m, a0o, a1m, a1o, a2m, a2o, a3m, a3o, o0, o1, o2, o3):
    f2, f3 = flag[0] == 1, flag[1] == 1
    n = a0m.shape[1]

    def block(g, i):
        halves = [
            g[h * 16:(h + 1) * 16, i * PIECE:(i + 1) * PIECE, :].reshape(n, 128) for h in range(2)
        ]
        return jnp.concatenate(halves, axis=1)

    a2f = jnp.where(f2, a2o[...], a2m[...])
    a3f = jnp.where(f3, a3o[...], a3m[...])
    a0f2 = jnp.where(f2, a0o[...], a0m[...])
    a0f3 = jnp.where(f3, a0o[...], a0m[...])
    a2f3 = jnp.where(f3, a2o[...], a2m[...])
    own4, own5, own6 = block(gm, 4), block(gm, 5), block(gm, 6)
    got4 = jnp.where(f2, block(go, 4), own4)
    got5 = jnp.where(f3, block(go, 5), own5)
    got6 = jnp.where(f3, block(go, 6), own6)
    g0, g1, g2, g3 = [block(gm, i) for i in range(4)]
    o0[...] = (
        dot(a0m[...], block(gm, 7), 1, 0)
        + dot(a0o[...], block(gm, 8), 1, 1)
        + dot(a1m[...], g0, 1, 0)
        + dot(a1o[...], block(go, 1), 1, 0)
        + dot(a2f, own4, 1, 1)
        + dot(a3f, own5, 1, 1)
    )
    o1[...] = (
        dot(a0m[...], g0, 1, 1)
        + dot(a0o[...], g1, 1, 1)
        + dot(a3m[...], g2, 1, 1)
        + dot(a3o[...], g3, 1, 1)
    ).astype(bf16)
    o2[...] = (dot(a0f2, got4, 1, 0) + dot(a3f, own6, 1, 1)).astype(bf16)
    o3[...] = (
        dot(a1m[...], g2, 1, 0)
        + dot(a1o[...], block(go, 3), 1, 0)
        + dot(a0f3, got5, 1, 0)
        + dot(a2f3, got6, 1, 0)
    ).astype(bf16)


def call(kernel, outs, ops, flops):
    whole = pl.BlockSpec(memory_space=pltpu.VMEM)
    nbytes = sum(math.prod(v.shape) * v.dtype.itemsize for v in list(outs) + list(ops))
    return pl.pallas_call(
        kernel,
        out_shape=outs,
        in_specs=[pl.BlockSpec(memory_space=pltpu.SMEM)] + [whole] * (len(ops) - 1),
        out_specs=[whole] * len(outs),
        compiler_params=pltpu.CompilerParams(vmem_limit_bytes=24 * 2**20),
        cost_estimate=pl.CostEstimate(flops=flops, bytes_accessed=nbytes, transcendentals=0),
    )(*ops)


def gather(own):
    q1 = shift(own, "x", X, -1)
    q3 = shift(own, "yl", YL, 1)
    q2 = shift(own, "x", X, 2)
    swap = lambda v: shift(v, "core", CORE, 1)
    return [own, swap(own), q1, swap(q1), q2, swap(q2), q3, swap(q3)]


def apply_gram(flag, gm, go, parts):
    k, n = parts[0].shape
    outs = [jax.ShapeDtypeStruct((k, n), f32)] + [jax.ShapeDtypeStruct((k, n), bf16)] * 3
    o0, o1, o2, o3 = call(apply_kernel, outs, [flag, gm, go] + parts, 2 * 16 * k * n * n)
    r1 = shift(o1, "x", X, 1)
    r3 = shift(o3, "yl", YL, 1)
    r2 = shift(o2, "x", X, 2)
    return o0 + (r1.astype(f32) + r3.astype(f32) + r2.astype(f32))


def on_device(iterate):
    own = iterate.T
    k, n = own.shape
    scale = 0.2 * math.sqrt(max(n * X * YL * CORE, k * YH * Z))
    flag = jnp.stack([lax.axis_index("x") // 2, lax.axis_index("yl")]).astype(jnp.int32)
    parts = gather(own)
    a0m, a0o, a1m, a1o, a2m, a2o, a3m, a3o = parts
    shape = jax.ShapeDtypeStruct((YH * Z, BLOCKS * PIECE, 128), bf16)
    pieces = call(gram_kernel, [shape], [flag, a0m, a0o, a1m, a2m, a2o, a3m, a3o], 2 * 9 * k * n * n)[0]
    pieces = lax.all_to_all(pieces, COL, 0, 0)
    tile = pieces.astype(f32).sum(0).astype(bf16)
    gm = lax.all_to_all(jnp.broadcast_to(tile[None], shape.shape), COL, 0, 0)
    go = shift(gm, "core", CORE, 1)
    b = apply_gram(flag, gm, go, parts)
    d = (coef_cubic * own.astype(f32) + coef_quintic * b).astype(bf16)
    c = apply_gram(flag, gm, go, gather(d))
    return (scale * (coef_linear * own.astype(f32) + c)).astype(bf16).T


def solution(mesh):
    fine = Mesh(mesh.devices.reshape(X, YL, CORE, YH, Z), ("x", "yl", "core", "yh", "z"))
    spec = P(("x", "yl", "core"), ("yh", "z"))
    return jax.shard_map(on_device, mesh=fine, in_specs=(spec,), out_specs=spec, check_vma=False)
```
